512 devices in a mesh: member: 64 (over z, y_hi, core), tensor: 8 (over y_lo, x).
Axes of the slice: x: 4, y: 4 (y_hi: 2, y_lo: 2; y = y_hi * 2 + y_lo), z: 16, core: 2. Of those that a mesh axis runs over, the one named last changes fastest.
Arguments:
- inputs: bfloat16 [1024, 5120], P('member', 'tensor'), may hold values from -6 to 6
- key_weight: bfloat16 [5120, 20480], P('tensor', 'member'), may hold values from -0.078125 to 0.078125
- value_weight: bfloat16 [20480, 5120], P('member', 'tensor'), may hold values from -0.0390625 to 0.0390625
- key_probe: bfloat16 [1024, 5120], P('member', 'tensor'), may hold values from -6 to 6
- key_spread: bfloat16 [1024, 20480], P('tensor', 'member'), may hold values from -6 to 6
- value_probe: bfloat16 [1024, 20480], P('tensor', 'member'), may hold values from -6 to 6
- value_spread: bfloat16 [1024, 5120], P('member', 'tensor'), may hold values from -6 to 6
- fitness: bfloat16 [1024], P('member'), may hold values from -6 to 6
Outputs:
- outputs: bfloat16 [1024, 5120], P('member', 'tensor')
- key_update: bfloat16 [5120, 20480], P('tensor', 'member')
- value_update: bfloat16 [20480, 5120], P('member', 'tensor')
The draws below stay inside these ranges and needn't reach their ends.
All inputs are finite; a program needn't handle non-finite values.
Results may differ from the reference program's by a relative error of at most 0.0065.
Values may be sent and summed in bfloat16 or wider, within the bound.
A program may use at most 64 MiB of HBM per device.

```python
import math
import jax
import jax.numpy as jnp
from jax import lax

D = 5120
FF = 20480
MEMBERS = 1024


def levels(rng, extent, pieces, low, top_value):
    loudness = 1.0
    for position, blocks in pieces:
        heights = jax.random.uniform(jax.random.fold_in(jax.random.fold_in(rng, 6), position), (blocks,), jnp.float32, low / len(pieces), top_value / len(pieces))
        loudness = loudness * jnp.repeat(jnp.exp(heights), extent[position] // blocks).reshape((-1,) + (1,) * (len(extent) - 1 - position))
    return loudness


def noise(own_key, extent, deviation, most, pieces=(), held_as=jnp.bfloat16):
    level = levels(own_key, extent, pieces, -0.22, 0.18) if pieces else 1.0
    drawn = jax.random.normal(own_key, extent, jnp.float32) * deviation * level
    return jnp.minimum(jnp.maximum(drawn, -most), most).astype(held_as)


def setup_inputs(seed: int = 0) -> dict:
    streams_of = jax.random.split(jax.random.key(seed), 9)
    return {
        "inputs": noise(streams_of[0], (MEMBERS, D), 1.0, 6.0, ((0, 64), (1, 8))),
        "key_weight": noise(streams_of[1], (D, FF), D ** -0.5, 0.078125, ((0, 8), (1, 64))),
        "value_weight": noise(streams_of[2], (FF, D), FF ** -0.5, 0.0390625, ((0, 64), (1, 8))),
        "key_probe": noise(streams_of[3], (MEMBERS, D), 1.0, 6.0, ((0, 64), (1, 8))),
        "key_spread": noise(streams_of[4], (MEMBERS, FF), 1.0, 6.0, ((0, 8), (1, 64))),
        "value_probe": noise(streams_of[5], (MEMBERS, FF), 1.0, 6.0, ((0, 8), (1, 64))),
        "value_spread": noise(streams_of[6], (MEMBERS, D), 1.0, 6.0, ((0, 64), (1, 8))),
        "fitness": noise(streams_of[7], (MEMBERS,), 1.0, 6.0, ((0, 64),)),
    }


sigma_scale = 0.005

def reference(inputs, key_weight, value_weight, key_probe, key_spread, value_probe, value_spread, fitness):
    key_dots = lax.optimization_barrier(jnp.sum(inputs.astype(jnp.float32) * key_probe.astype(jnp.float32), axis=1))
    key_pre = jnp.dot(inputs, key_weight, preferred_element_type=jnp.float32) + sigma_scale * key_dots[:, None] * key_spread.astype(jnp.float32)
    hidden = (jnp.maximum(key_pre, 0.0) ** 2).astype(jnp.bfloat16)
    value_dots = lax.optimization_barrier(jnp.sum(hidden.astype(jnp.float32) * value_probe.astype(jnp.float32), axis=1))
    outputs = (jnp.dot(hidden, value_weight, preferred_element_type=jnp.float32) + sigma_scale * value_dots[:, None] * value_spread.astype(jnp.float32)).astype(jnp.bfloat16)
    factor = fitness.astype(jnp.float32)[:, None] * (1.0 / math.sqrt(MEMBERS))
    weighted_key = (factor * key_spread.astype(jnp.float32)).astype(jnp.bfloat16)
    key_update = lax.dot_general(key_probe, weighted_key, (((0,), (0,)), ((), ())), preferred_element_type=jnp.float32).astype(jnp.bfloat16)
    weighted_value = (factor * value_spread.astype(jnp.float32)).astype(jnp.bfloat16)
    value_update = lax.dot_general(value_probe, weighted_value, (((0,), (0,)), ((), ())), preferred_element_type=jnp.float32).astype(jnp.bfloat16)
    return (outputs, key_update, value_update)
```

```python
import functools

import jax
import jax.numpy as jnp
from jax import lax
from jax.experimental import pallas as pl
from jax.experimental.pallas import tpu as pltpu
from jax.sharding import PartitionSpec as P

BF, F32 = jnp.bfloat16, jnp.float32
MESH = pl.DeviceIdType.MESH
SIGMA = 0.005

FAR = (4, -4, 8)
NEAR = (
    (1, 0), (-1, 0), (2, 0), (-2, 0),
    (1, -4), (-1, -4), (2, -4),
    (1, 4), (-1, 4), (-2, 4),
    (1, 8), (-1, 8),
)
OFFSETS = (0, -1, 1, -2, 2, -4, 4, -5, 3, -3, 5, -6, 6, 8, 7, -7)


def kernel(
    x_ref, kw_ref, vw_ref, kp_ref, ks_ref, vp_ref, vs_ref, f_ref,
    out_ref, ku_ref, vu_ref,
    gi, gr, ksa, vpa, bsend, rsb, hid, wgt_k, wgt_v, pbuf, psend, rsib, ysend, ry, zf, zb, rn, rn2, fb, rf,
    zs, zr, ys, yr, cs, cr, zs2, zr2, ys2, yr2, cs2, cr2, ts, tr, s_core, r_core, s_y, r_y, s_z, r_z, s_f, r_f,
):
    m, t = lax.axis_index("member"), lax.axis_index("tensor")
    z, half, core = m // 4, (m // 2) % 2, m % 2
    other, sib = 1 - half, 1 - core

    def at_z(dz):
        return (lax.rem(z + dz + 16, 16) * 4 + half * 2 + core, t)

    y_dev = (z * 4 + other * 2 + core, t)
    c_dev = (z * 4 + half * 2 + sib, t)

    def tau(tt):
        return lax.rem(tt, 2) * 4 + tt // 2

    def slot(dz):
        zz = lax.rem(z + dz + 16, 16)
        return (lax.rem(zz, 4) // 2) * 4 + zz // 4, lax.rem(zz, 2)

    def klass(r):
        cc = lax.rem(z + r, 4)
        return pl.ds((cc // 2) * 4, 4), lax.rem(cc, 2)

    me_tau = tau(t)
    pending = []

    def copy(src, dst, ssem, rsem, dev):
        return pltpu.make_async_remote_copy(
            src_ref=src, dst_ref=dst, send_sem=ssem, recv_sem=rsem, device_id=dev, device_id_type=MESH
        )

    def send(src, dst, ssem, rsem, dev):
        c = copy(src, dst, ssem, rsem, dev)
        c.start()
        pending.append(c)

    def arrive(dst, ssem, rsem, dev):
        copy(dst, dst, ssem, rsem, dev).wait_recv()

    bar = pltpu.get_barrier_semaphore()
    partners = [at_z(d) for d in (1, -1, 2, -2, 4, -4, 8)] + [y_dev, c_dev]
    partners += [(m, lax.rem(t + k, 8)) for k in range(1, 8)]
    for dev in partners:
        pl.semaphore_signal(bar, inc=1, device_id=dev, device_id_type=MESH)

    fit = jnp.broadcast_to(f_ref[...].astype(F32), (16, 16))
    row, lane = (lax.broadcasted_iota(jnp.int32, (16, 16), d) for d in (0, 1))
    fit = jnp.sum(jnp.where(row == lane, fit, 0.0), axis=1, keepdims=True)
    dots = jnp.sum(x_ref[...].astype(F32) * kp_ref[...].astype(F32), axis=1, keepdims=True)
    high = dots.astype(BF).astype(F32)
    lanes = lax.broadcasted_iota(jnp.int32, (16, 128), 1)
    aux = jnp.where(lanes == 0, high, jnp.where(lanes == 1, dots - high, jnp.where(lanes == 2, fit, 0.0)))
    st, sl = slot(0)
    gi[st, sl, half, core, :, 0:640] = x_ref[...]
    gi[st, sl, half, core, :, 640:768] = aux.astype(BF)
    gr[st, sl, half, core, :, 0:640] = kp_ref[...]
    gr[st, sl, half, core, :, 640:1280] = vs_ref[...]
    ksa[me_tau] = ks_ref[...]
    vpa[me_tau] = vp_ref[...]

    pl.semaphore_wait(bar, len(partners))

    def chunk(g, dz, hh=None, cc=None):
        a, b = slot(dz)
        return g.at[a, b, half if hh is None else hh, core if cc is None else cc]

    def block(g, r, hh, cc):
        a, b = klass(r)
        return g.at[a, b, hh, cc]

    def far_send(g, s, r):
        for k, d in enumerate(FAR):
            send(chunk(g, 0), chunk(g, 0), s.at[k], r.at[k], at_z(d))

    def near_send(g, s, r, o):
        for k, (d, oo) in enumerate(NEAR):
            if oo == o:
                send(chunk(g, o), chunk(g, o), s.at[3 + k], r.at[3 + k], at_z(d))

    def far_wait(g, s, r, k):
        arrive(chunk(g, -FAR[k]), s.at[k], r.at[k], at_z(-FAR[k]))

    def near_wait(g, s, r, o, then=None):
        for k, (d, oo) in enumerate(NEAR):
            if oo == o:
                arrive(chunk(g, oo - d), s.at[3 + k], r.at[3 + k], at_z(-d))
                if then is not None:
                    then(oo - d)

    def y_send(dz):
        dz = dz if dz <= 8 else dz - 16
        k = OFFSETS.index(dz)
        send(chunk(gi, dz), chunk(gi, dz), ys.at[k], yr.at[k], y_dev)

    far_send(gi, zs, zr)
    near_send(gi, zs, zr, 0)
    y_send(0)
    far_send(gr, zs2, zr2)
    near_send(gr, zs2, zr2, 0)

    def spread(buf, base):
        for k in range(1, 8):
            dev = (m, lax.rem(t + k, 8))
            send(buf.at[me_tau], buf.at[me_tau], ts.at[base + k], tr.at[base + k], dev)

    def spread_wait(buf, base):
        for k in range(1, 8):
            frm = lax.rem(t + 8 - k, 8)
            arrive(buf.at[tau(frm)], ts.at[base + k], tr.at[base + k], (m, frm))

    spread(ksa, 0)

    near_wait(gi, zs, zr, 0, y_send)
    for k, o in ((0, -4), (1, 4)):
        far_wait(gi, zs, zr, k)
        near_send(gi, zs, zr, o)
        y_send(o)
    near_wait(gi, zs, zr, -4, y_send)
    near_wait(gi, zs, zr, 4, y_send)
    far_wait(gi, zs, zr, 2)
    near_send(gi, zs, zr, 8)
    y_send(8)
    near_wait(gi, zs, zr, 8, y_send)
    for r in range(4):
        send(block(gi, r, half, core), block(gi, r, half, core), cs.at[r], cr.at[r], c_dev)
    near_wait(gr, zs2, zr2, 0)
    for k, o in ((0, -4), (1, 4), (2, 8)):
        far_wait(gr, zs2, zr2, k)
        near_send(gr, zs2, zr2, o)
    for k, o in enumerate(OFFSETS):
        arrive(chunk(gi, o, other), ys.at[k], yr.at[k], y_dev)
    for r in range(4):
        send(block(gi, r, other, core), block(gi, r, other, core), cs.at[4 + r], cr.at[4 + r], c_dev)
    spread_wait(ksa, 0)
    for r in range(4):
        arrive(block(gi, r, half, sib), cs.at[r], cr.at[r], c_dev)
    for r in range(4):
        arrive(block(gi, r, other, sib), cs.at[4 + r], cr.at[4 + r], c_dev)

    def key_block(tt):
        rows = gi[tt].reshape(128, 768)
        tail = rows[:, 640:768].astype(F32)
        dp = (tail[:, 0:1] + tail[:, 1:2]) * SIGMA
        part = jnp.dot(rows[:, 0:640], kw_ref[...], preferred_element_type=F32)
        return (part + dp * ksa[tt].astype(F32)).astype(BF)

    def key_step(k, carry):
        tgt = lax.rem(t + k, 8)
        tt = tau(tgt)
        bsend[k] = key_block(tt)
        copy(bsend.at[k], rsb.at[me_tau], ts.at[8 + k], tr.at[8 + k], (m, tgt)).start()
        return carry

    lax.fori_loop(1, 8, key_step, 0)
    rsb[me_tau] = key_block(me_tau)

    near_wait(gr, zs2, zr2, -4)
    near_wait(gr, zs2, zr2, 4)
    near_wait(gr, zs2, zr2, 8)
    for r in range(4):
        send(block(gr, r, half, core), block(gr, r, half, core), ys2.at[r], yr2.at[r], y_dev)
        send(block(gr, r, half, core), block(gr, r, half, core), cs2.at[r], cr2.at[r], c_dev)

    spread_wait(rsb, 8)
    pre = rsb[0].astype(F32)
    for k in range(1, 8):
        pre = pre + rsb[k].astype(F32)
    act = jnp.maximum(pre, 0.0)
    act = (act * act).astype(BF)
    vd = jnp.sum(act.astype(F32) * vp_ref[...].astype(F32), axis=1, keepdims=True)
    vhigh = vd.astype(BF).astype(F32)
    lanes = lax.broadcasted_iota(jnp.int32, (128, 64), 1)
    tail = jnp.where(lanes == 0, vhigh, jnp.where(lanes == 1, vd - vhigh, 0.0)).astype(BF)
    hid[me_tau] = jnp.concatenate([act, tail], axis=1)
    spread(hid, 16)
    spread(vpa, 24)

    for r in range(4):
        arrive(block(gr, r, other, core), ys2.at[r], yr2.at[r], y_dev)
        send(block(gr, r, other, core), block(gr, r, other, core), cs2.at[4 + r], cr2.at[4 + r], c_dev)
    for r in range(4):
        arrive(block(gr, r, half, sib), cs2.at[r], cr2.at[r], c_dev)
    for r in range(4):
        arrive(block(gr, r, other, sib), cs2.at[4 + r], cr2.at[4 + r], c_dev)

    def weigh(b, carry):
        fcol = gi[b].reshape(128, 768)[:, 640:768].astype(F32)[:, 2:3] * (1.0 / 32.0)
        wgt_k[b] = (fcol * ksa[b].astype(F32)).astype(BF)
        wgt_v[b] = (fcol * gr[b].reshape(128, 1280)[:, 640:1280].astype(F32)).astype(BF)
        return carry

    lax.fori_loop(0, 8, weigh, 0)

    def outer(left, right):
        return lax.dot_general(left, right, (((0,), (0,)), ((), ())), preferred_element_type=F32).astype(BF)

    for j in range(5):
        left = gr[:, :, :, :, :, j * 128 : (j + 1) * 128].reshape(1024, 128)
        ku_ref[j * 128 : (j + 1) * 128, :] = outer(left, wgt_k[...].reshape(1024, 320))

    spread_wait(hid, 16)

    def value_step(b, carry):
        rows = hid[b]
        vd = (rows[:, 320:321].astype(F32) + rows[:, 321:322].astype(F32)) * SIGMA
        part = jnp.dot(rows[:, 0:320], vw_ref[...], preferred_element_type=F32)
        part = part + vd * gr[b].reshape(128, 1280)[:, 640:1280].astype(F32)
        pbuf[b] = part.reshape(2, 2, 2, 16, 640)
        psend[b] = pbuf[b, :, :, sib].astype(BF)
        copy(psend.at[b], rsib.at[b], s_core.at[b], r_core.at[b], c_dev).start()
        return carry

    lax.fori_loop(0, 8, value_step, 0)

    def y_step(b, carry):
        arrive(rsib.at[b], s_core.at[b], r_core.at[b], c_dev)
        ysend[b] = (pbuf[b, :, other, core] + rsib[b, :, other].astype(F32)).astype(BF)
        copy(ysend.at[b], ry.at[b], s_y.at[b], r_y.at[b], y_dev).start()
        return carry

    lax.fori_loop(0, 8, y_step, 0)

    def z_step(b, carry):
        arrive(ry.at[b], s_y.at[b], r_y.at[b], y_dev)
        total = pbuf[b, :, half, core] + rsib[b, :, half].astype(F32) + ry[b].astype(F32)
        zf[b] = total
        zb[b] = total.astype(BF)
        return carry

    lax.fori_loop(0, 8, z_step, 0)

    for k, d in enumerate((1, -1)):
        a, b = klass(d + 4)
        send(zb.at[a, b], rn.at[k], s_z.at[k], r_z.at[k], at_z(d))
    for k, d in enumerate((2, -2)):
        for j, w in enumerate((d, 3 * d)):
            a, b = slot(w)
            i = 2 + 2 * k + j
            send(zb.at[a, b], rn2.at[k, j], s_z.at[i], r_z.at[i], at_z(d))

    spread_wait(vpa, 24)
    right = wgt_v[...].reshape(1024, 640)
    for a, b in ((0, 128), (128, 256), (256, 320)):
        vu_ref[a:b, :] = outer(vpa[:, :, a:b].reshape(1024, b - a), right)

    for k, d in enumerate((1, -1)):
        arrive(rn.at[k], s_z.at[k], r_z.at[k], at_z(-d))
    for k, d in enumerate((2, -2)):
        for j in range(2):
            i = 2 + 2 * k + j
            arrive(rn2.at[k, j], s_z.at[i], r_z.at[i], at_z(-d))

    def gathered(dz):
        a, b = slot(dz)
        za = lax.rem(a, 4)
        return zf[a, b] + rn[0, za].astype(F32) + rn[1, za].astype(F32)

    for k, d in enumerate(FAR):
        total = gathered(d)
        if k < 2:
            total = total + rn2[k, 1].astype(F32)
        fb[k] = total.astype(BF)
        send(fb.at[k], rf.at[k], s_f.at[k], r_f.at[k], at_z(d))
    total = gathered(0) + rn2[0, 0].astype(F32) + rn2[1, 0].astype(F32)
    for k, d in enumerate(FAR):
        arrive(rf.at[k], s_f.at[k], r_f.at[k], at_z(-d))
        total = total + rf[k].astype(F32)
    out_ref[...] = total.astype(BF)

    for c in pending:
        c.wait_send()
    for k in range(1, 8):
        copy(bsend.at[k], rsb.at[me_tau], ts.at[8 + k], tr.at[8 + k], (m, lax.rem(t + k, 8))).wait_send()
    for b in range(8):
        copy(psend.at[b], rsib.at[b], s_core.at[b], r_core.at[b], c_dev).wait_send()
        copy(ysend.at[b], ry.at[b], s_y.at[b], r_y.at[b], y_dev).wait_send()


def body(*args):
    *rest, fitness = args
    vm = pl.BlockSpec(memory_space=pltpu.VMEM)
    dma = pltpu.SemaphoreType.DMA
    return pl.pallas_call(
        kernel,
        out_shape=(
            jax.ShapeDtypeStruct((16, 640), BF),
            jax.ShapeDtypeStruct((640, 320), BF),
            jax.ShapeDtypeStruct((320, 640), BF),
        ),
        in_specs=[vm] * 8,
        out_specs=(vm, vm, vm),
        scratch_shapes=[
            pltpu.VMEM((8, 2, 2, 2, 16, 768), BF),
            pltpu.VMEM((8, 2, 2, 2, 16, 1280), BF),
            pltpu.VMEM((8, 128, 320), BF),
            pltpu.VMEM((8, 128, 320), BF),
            pltpu.VMEM((8, 128, 320), BF),
            pltpu.VMEM((8, 128, 320), BF),
            pltpu.VMEM((8, 128, 384), BF),
            pltpu.VMEM((8, 128, 320), BF),
            pltpu.VMEM((8, 128, 640), BF),
            pltpu.VMEM((8, 2, 2, 2, 16, 640), F32),
            pltpu.VMEM((8, 2, 2, 16, 640), BF),
            pltpu.VMEM((8, 2, 2, 16, 640), BF),
            pltpu.VMEM((8, 2, 16, 640), BF),
            pltpu.VMEM((8, 2, 16, 640), BF),
            pltpu.VMEM((8, 2, 16, 640), F32),
            pltpu.VMEM((8, 2, 16, 640), BF),
            pltpu.VMEM((2, 4, 16, 640), BF),
            pltpu.VMEM((2, 2, 16, 640), BF),
            pltpu.VMEM((3, 16, 640), BF),
            pltpu.VMEM((3, 16, 640), BF),
        ]
        + [dma((n,)) for n in (15, 15, 16, 16, 8, 8, 15, 15, 4, 4, 8, 8, 32, 32, 8, 8, 8, 8, 6, 6, 3, 3)],
        compiler_params=pltpu.CompilerParams(
            collective_id=0, has_side_effects=True, vmem_limit_bytes=48 * 2**20
        ),
        cost_estimate=pl.CostEstimate(flops=1_700_000_000, bytes_accessed=4_000_000, transcendentals=0),
        name="step",
    )(*rest, fitness.reshape(1, 16))


def solution(mesh):
    placed = (
        P("member", "tensor"), P("tensor", "member"), P("member", "tensor"), P("member", "tensor"),
        P("tensor", "member"), P("tensor", "member"), P("member", "tensor"), P("member"),
    )
    return jax.shard_map(
        body,
        mesh=mesh,
        in_specs=placed,
        out_specs=(P("member", "tensor"), P("tensor", "member"), P("member", "tensor")),
        check_vma=False,
    )
```

```python
import functools

import jax
import jax.numpy as jnp
from jax import lax
from jax.experimental import pallas as pl
from jax.experimental.pallas import tpu as pltpu
from jax.sharding import PartitionSpec as P

BF, F32 = jnp.bfloat16, jnp.float32
MESH = pl.DeviceIdType.MESH
SIGMA = 0.005

FAR = (4, -4, 8)
NEAR = (
    (1, 0), (-1, 0), (2, 0), (-2, 0),
    (1, -4), (-1, -4), (2, -4),
    (1, 4), (-1, 4), (-2, 4),
    (1, 8), (-1, 8),
)
OFFSETS = (0, -1, 1, -2, 2, -4, 4, -5, 3, -3, 5, -6, 6, 8, 7, -7)


def kernel(
    x_ref, kw_ref, vw_ref, kp_ref, ks_ref, vp_ref, vs_ref, f_ref,
    out_ref, ku_ref, vu_ref,
    kw, vw, fv, vsv, gi, gr, ksa, vpa, bsend, rsb, hid, wgt_k, pbuf, psend, rsib, ysend, ry, zf, zb, rn, rn2, fb, rf, vdt, vds, vdr, mt, mts, mtr,
    ls, zs, zr, ys, yr, cs, cr, gs, gv, ys2, yr2, cs2, cr2, ts, tr, s_core, r_core, s_y, r_y, s_z, r_z, s_f, r_f, s_vd, r_vd, s_mt, r_mt,
):
    m, t = lax.axis_index("member"), lax.axis_index("tensor")
    z, half, core = m // 4, (m // 2) % 2, m % 2
    other, sib = 1 - half, 1 - core

    def at_z(dz):
        return (lax.rem(z + dz + 16, 16) * 4 + half * 2 + core, t)

    y_dev = (z * 4 + other * 2 + core, t)
    c_dev = (z * 4 + half * 2 + sib, t)

    def tau(tt):
        return lax.rem(tt, 2) * 4 + tt // 2

    def slot(dz):
        zz = lax.rem(z + dz + 16, 16)
        return (lax.rem(zz, 4) // 2) * 4 + zz // 4, lax.rem(zz, 2)

    def klass(r):
        cc = lax.rem(z + r, 4)
        return pl.ds((cc // 2) * 4, 4), lax.rem(cc, 2)

    def cols(tt):
        return pl.ds(pl.multiple_of(tt * 128, 128), 128)

    parts = (pl.ds(0, 160), pl.ds(160, 176))

    def at_block(buf, tt, part=None):
        if buf is vpa:
            return buf.at[:, cols(tt)]
        return buf.at[tt] if part is None else buf.at[tt, parts[part]]

    me_tau = tau(t)
    pending = []

    def copy(src, dst, ssem, rsem, dev):
        return pltpu.make_async_remote_copy(
            src_ref=src, dst_ref=dst, send_sem=ssem, recv_sem=rsem, device_id=dev, device_id_type=MESH
        )

    def send(src, dst, ssem, rsem, dev):
        c = copy(src, dst, ssem, rsem, dev)
        c.start()
        pending.append(c)

    def arrive(dst, ssem, rsem, dev):
        copy(dst, dst, ssem, rsem, dev).wait_recv()

    bar = pltpu.get_barrier_semaphore()
    partners = [at_z(d) for d in (8, 4, -4, 1, -1, 2, -2)] + [y_dev, c_dev]
    partners += [(m, lax.rem(t + k, 8)) for k in range(1, 8)]
    for dev in partners:
        pl.semaphore_signal(bar, inc=1, device_id=dev, device_id_type=MESH)

    def chunk(g, dz, hh=None, cc=None):
        a, b = slot(dz)
        return g.at[a, b, half if hh is None else hh, core if cc is None else cc]

    def block(g, r, hh, cc):
        a, b = klass(r)
        return g.at[a, b, hh, cc]

    st, sl = slot(0)
    mine_i, mine_r = gi.at[st, sl, half, core], gr.at[st, sl, half, core]
    loads = [
        pltpu.make_async_copy(src, dst, ls.at[k])
        for k, (src, dst) in enumerate(
            (
                (x_ref, mine_i), (kp_ref, mine_r.at[:, 0:640]), (vs_ref, vsv),
                (ks_ref, ksa.at[me_tau]), (vp_ref, vpa.at[:, cols(me_tau)]), (f_ref, fv), (kw_ref, kw), (vw_ref, vw),
            )
        )
    ]
    for c in loads:
        c.start()

    first = sl * 64 + half * 32 + core * 16
    spot = lax.broadcasted_iota(jnp.int32, (16, 128), 1) == first + lax.broadcasted_iota(jnp.int32, (16, 128), 0)

    def place(col):
        return jnp.sum(jnp.where(spot, col, 0.0), axis=0, keepdims=True)

    mt[...] = jnp.zeros((16, 128), F32)
    for c in loads[0:6]:
        c.wait()
    fit = jnp.broadcast_to(fv[...].astype(F32), (16, 16))
    row, lane = (lax.broadcasted_iota(jnp.int32, (16, 16), d) for d in (0, 1))
    fit = jnp.sum(jnp.where(row == lane, fit, 0.0), axis=1, keepdims=True) * (1.0 / 32.0)
    dots = jnp.sum(mine_i[...].astype(F32) * mine_r[:, 0:640].astype(F32), axis=1, keepdims=True)
    mt[pl.ds(st, 1)] = place(dots * SIGMA)
    mt[pl.ds(8 + st, 1)] = place(fit)
    mine_r[:, 640:1280] = (fit * vsv[...].astype(F32)).astype(BF)

    pl.semaphore_wait(bar, len(partners))

    def near_send(o):
        for k, (d, oo) in enumerate(NEAR):
            if oo == o:
                send(chunk(gi, o), chunk(gi, o), zs.at[3 + k], zr.at[3 + k], at_z(d))

    def far_wait(k):
        arrive(chunk(gi, -FAR[k]), zs.at[k], zr.at[k], at_z(-FAR[k]))

    def near_wait(o):
        for k, (d, oo) in enumerate(NEAR):
            if oo == o:
                arrive(chunk(gi, oo - d), zs.at[3 + k], zr.at[3 + k], at_z(-d))
                y_send(oo - d)

    def y_send(dz):
        dz = dz if dz <= 8 else dz - 16
        k = OFFSETS.index(dz)
        send(chunk(gi, dz), chunk(gi, dz), ys.at[k], yr.at[k], y_dev)

    ty = lax.rem(t + 4, 8)

    def along_x(k):
        return (t // 4) * 4 + lax.rem(t + k, 4)

    def source(k):
        return lax.rem((t // 4) * 4 + lax.rem(t + 4 - lax.rem(k, 4), 4) + 4 * (k // 4), 8)

    def spread(buf, base, part=None):
        b = at_block(buf, me_tau, part)
        send(b, b, ts.at[base + 4], tr.at[base + 4], (m, ty))
        for k in (2, 1, 3):
            send(b, b, ts.at[base + k], tr.at[base + k], (m, along_x(k)))

    def pass_on(buf, base, part=None, to=(2, 1, 3)):
        b = at_block(buf, tau(ty), part)
        arrive(b, ts.at[base + 4], tr.at[base + 4], (m, ty))
        for k in to:
            send(b, b, ts.at[base + 4 + k], tr.at[base + 4 + k], (m, along_x(k)))

    def pass_back(buf, base, part):
        spread_wait(buf, base, 2, part)
        b = at_block(buf, tau(along_x(2)), part)
        send(b, b, ts.at[base + 6], tr.at[base + 6], (m, ty))

    def spread_wait(buf, base, k, part=None):
        frm = source(k)
        arrive(at_block(buf, tau(frm), part), ts.at[base + k], tr.at[base + k], (m, frm))

    def ring_send(s):
        for hh in (0, 1):
            for sign in (1, -1):
                if s == 8 and (hh == 0) != (sign > 0):
                    continue
                i = (sign < 0) * 16 + (s - 1) * 2 + hh
                c = chunk(gr, -sign * (s - 1), hh)
                send(c, c, gs.at[i], gv.at[i], at_z(sign))

    def ring_wait(s):
        for hh in (0, 1):
            for sign in (1, -1):
                if s == 8 and (hh == 0) != (sign > 0):
                    continue
                i = (sign < 0) * 16 + (s - 1) * 2 + hh
                c = chunk(gr, -sign * s, hh)
                arrive(c, gs.at[i], gv.at[i], at_z(-sign))
                if s < 7 or (s == 7 and (hh == 0) == (sign > 0)):
                    n = i + 2
                    send(c, c, gs.at[n], gv.at[n], at_z(sign))
                send(c, c, cs2.at[i], cr2.at[i], c_dev)

    def ring_end():
        for s in range(1, 9):
            for hh in (0, 1):
                for sign in (1, -1):
                    if s == 8 and (hh == 0) != (sign > 0):
                        continue
                    i = (sign < 0) * 16 + (s - 1) * 2 + hh
                    arrive(chunk(gr, -sign * s, hh, sib), cs2.at[i], cr2.at[i], c_dev)
        for hh in (0, 1):
            arrive(chunk(gr, 0, hh, sib), cs2.at[32 + hh], cr2.at[32 + hh], c_dev)

    def round_of(tile, held, got, ssem, rsem):
        def begin(n, *links):
            held[n] = tile[...]
            for k, dev in links:
                send(held.at[n], got.at[k], ssem.at[k], rsem.at[k], dev)

        def end(*ks):
            for k in ks:
                arrive(got.at[k], ssem.at[k], rsem.at[k], c_dev)
                tile[...] += got[k]

        return begin, end

    mt_send, mt_add = round_of(mt, mts, mtr, s_mt, r_mt)
    vd_send, vd_add = round_of(vdt, vds, vdr, s_vd, r_vd)
    near_links = ((2, at_z(1)), (3, at_z(-1)), (4, at_z(-2)))
    far_links = ((5, at_z(4)), (6, at_z(-4)), (7, at_z(8)))

    mt_send(0, *far_links)
    for k in (2, 0, 1):
        send(chunk(gi, 0), chunk(gi, 0), zs.at[k], zr.at[k], at_z(FAR[k]))
    near_send(0)
    y_send(0)
    send(mine_r, mine_r, ys2, yr2, y_dev)
    spread(ksa, 0)

    for k, o in ((0, -4), (1, 4)):
        far_wait(k)
        near_send(o)
    near_wait(0)
    for o in (-4, 4):
        y_send(o)
    far_wait(2)
    near_send(8)
    y_send(8)
    mt_add(5, 6, 7)
    mt_send(1, *near_links)
    theirs = chunk(gr, 0, other)
    arrive(theirs, ys2, yr2, y_dev)
    ring_send(1)
    for hh in (0, 1):
        c = chunk(gr, 0, hh)
        send(c, c, cs2.at[32 + hh], cr2.at[32 + hh], c_dev)
    pass_on(ksa, 0)
    near_wait(-4)
    near_wait(4)
    near_wait(8)
    mt_add(2, 3, 4)
    mt_send(2, (1, y_dev))
    for r in range(4):
        send(block(gi, r, half, core), block(gi, r, half, core), cs.at[r], cr.at[r], c_dev)
    ring_wait(1)
    for r in range(4):
        for o in OFFSETS:
            if (o - r) % 4 == 0:
                k = OFFSETS.index(o)
                arrive(chunk(gi, o, other), ys.at[k], yr.at[k], y_dev)
        send(block(gi, r, other, core), block(gi, r, other, core), cs.at[4 + r], cr.at[4 + r], c_dev)
    mt_add(1)
    mt_send(3, (0, c_dev))
    for k in (1, 3, 2):
        spread_wait(ksa, 0, k)
        spread_wait(ksa, 0, k + 4)
    for c in loads[6:]:
        c.wait()
    for r in range(4):
        arrive(block(gi, r, half, sib), cs.at[r], cr.at[r], c_dev)
    for r in range(4):
        arrive(block(gi, r, other, sib), cs.at[4 + r], cr.at[4 + r], c_dev)

    mt_add(0)
    ring_wait(2)
    def key_block(tt):
        rows = gi[tt].reshape(128, 640)
        dp = mt[pl.ds(tt, 1)]
        part = lax.dot_general(
            kw[...], rows, (((1,), (1,)), ((), ())), preferred_element_type=F32
        )
        return (part + dp * ksa[tt].astype(F32)).astype(BF)

    def key_copy(k, h):
        tgt = lax.rem(t + k, 8)
        u = pl.ds(h * 160, 160)
        return copy(bsend.at[k, u], rsb.at[me_tau, u], ts.at[32 + 8 * h + k], tr.at[32 + 8 * h + k], (m, tgt))

    def key_step(i, carry):
        k = 7 - i
        bsend[k] = key_block(tau(lax.rem(t + k, 8)))
        key_copy(k, 0).start()
        return carry

    lax.fori_loop(0, 7, key_step, 0)
    for k in range(7, 0, -1):
        key_copy(k, 1).start()
    rsb[me_tau] = key_block(me_tau)

    def weigh_k(b, carry):
        wgt_k[:, cols(b)] = (mt[pl.ds(8 + b, 1)] * ksa[b].astype(F32)).astype(BF)
        return carry

    lax.fori_loop(0, 8, weigh_k, 0)
    ring_wait(3)
    def value_step(p, k):
        b = tau(source(k))
        tail = hid[b, 320:336].astype(F32)
        vdt[pl.ds(b, 1)] = tail[0:1] + tail[1:2]
        part = lax.dot_general(
            hid[b, 0:320], vw[...], (((0,), (0,)), ((), ())), preferred_element_type=F32
        )
        pbuf[p] = part.reshape(2, 2, 2, 16, 640)
        psend[p] = pbuf[p, :, :, sib].astype(BF)
        copy(psend.at[p], rsib.at[p], s_core.at[p], r_core.at[p], c_dev).start()

    def y_step(p):
        arrive(rsib.at[p], s_core.at[p], r_core.at[p], c_dev)
        ysend[p] = (pbuf[p, :, other, core] + rsib[p, :, other].astype(F32)).astype(BF)
        copy(ysend.at[p], ry.at[p], s_y.at[p], r_y.at[p], y_dev).start()

    def z_step(p, k):
        b = tau(source(k))
        arrive(ry.at[p], s_y.at[p], r_y.at[p], y_dev)
        total = pbuf[p, :, half, core] + rsib[p, :, half].astype(F32) + ry[p].astype(F32)
        zf[b] = total
        zb[b] = total.astype(BF)

    vd = jnp.zeros((1, 128), F32)
    for h in (0, 1):
        u = pl.ds(h * 160, 160)
        for k in range(1, 8):
            frm = lax.rem(t + 8 - k, 8)
            i = 32 + 8 * h + k
            arrive(rsb.at[tau(frm), u], ts.at[i], tr.at[i], (m, frm))
        pre = rsb[0, u].astype(F32)
        for k in range(1, 8):
            pre = pre + rsb[k, u].astype(F32)
        act = jnp.maximum(pre, 0.0)
        act = (act * act).astype(BF)
        hid[me_tau, u] = act
        vd = vd + jnp.sum(act.astype(F32) * vpa[u, cols(me_tau)].astype(F32), axis=0, keepdims=True)
        if h == 1:
            vhigh = vd.astype(BF).astype(F32)
            line = lax.broadcasted_iota(jnp.int32, (16, 128), 0)
            tail = jnp.where(line == 0, vhigh, jnp.where(line == 1, vd - vhigh, 0.0))
            hid[me_tau, 320:336] = tail.astype(BF)
        spread(hid, 8 + 8 * h, h)
        if h == 0:
            ring_wait(4)
    pass_on(hid, 8, 0, (1, 3))
    value_step(0, 0)
    ring_wait(5)
    pass_on(hid, 16, 1, (1, 3))
    pass_back(hid, 8, 0)
    value_step(1, 4)
    y_step(0)
    pass_back(hid, 16, 1)
    value_step(2, 2)
    y_step(1)

    def value_loop(p, carry):
        k = 2 * p - 5
        spread_wait(hid, 8, k, 0)
        spread_wait(hid, 16, k, 1)
        value_step(p, k)
        y_step(p - 1)
        return carry

    lax.fori_loop(3, 5, value_loop, 0)
    ring_wait(6)
    lax.fori_loop(5, 7, value_loop, 0)
    spread_wait(hid, 8, 6, 0)
    spread_wait(hid, 16, 6, 1)
    value_step(7, 6)
    y_step(6)
    vd_send(0, (0, c_dev))
    y_step(7)
    vd_add(0)
    vd_send(1, (1, y_dev))
    spread(vpa, 24)
    ring_wait(7)
    z_step(0, 0)
    z_step(1, 4)
    z_step(2, 2)

    def z_loop(p, carry):
        z_step(p, 2 * p - 5)
        return carry

    lax.fori_loop(3, 5, z_loop, 0)
    ring_wait(8)
    lax.fori_loop(5, 7, z_loop, 0)
    z_step(7, 6)

    spans = (pl.ds(0, 384), pl.ds(384, 256))

    def near_copies(c):
        w = spans[c]
        out = []
        for k, d in enumerate((1, -1)):
            a, b = klass(d + 4)
            out.append((zb.at[a, b, :, w], rn.at[k, :, :, w], d))
        for k, d in enumerate((2, -2)):
            for j, v in enumerate((d, 3 * d)):
                a, b = slot(v)
                out.append((zb.at[a, b, :, w], rn2.at[k, j, :, w], d))
        return out

    for c in (0, 1):
        for i, (src, dst, d) in enumerate(near_copies(c)):
            send(src, dst, s_z.at[6 * c + i], r_z.at[6 * c + i], at_z(d))
    vd_add(1)
    vd_send(2, *near_links)
    pass_on(vpa, 24)

    def gathered(dz, w):
        a, b = slot(dz)
        za = lax.rem(a, 4)
        return zf[a, b, :, w] + rn[0, za, :, w].astype(F32) + rn[1, za, :, w].astype(F32)

    def far_copy(k, c):
        w = spans[c]
        return fb.at[k, :, w], rf.at[k, :, w], s_f.at[3 * c + k], r_f.at[3 * c + k], at_z(FAR[k])

    for c in (0, 1):
        w = spans[c]
        for i, (_, dst, d) in enumerate(near_copies(c)):
            arrive(dst, s_z.at[6 * c + i], r_z.at[6 * c + i], at_z(-d))
        for k in (2, 0, 1):
            total = gathered(FAR[k], w)
            if k < 2:
                total = total + rn2[k, 1, :, w].astype(F32)
            fb[k, :, w] = total.astype(BF)
            send(*far_copy(k, c))
    vd_add(2, 3, 4)
    vd_send(3, *far_links)
    ring_end()

    def outer(left, right):
        return jnp.dot(left, right, preferred_element_type=F32).astype(BF)

    for a in range(0, 320, 64):
        ku_ref[a : a + 64] = outer(wgt_k[a : a + 64], gr[:, :, :, :, :, 0:640].reshape(1024, 640))
    for k in (1, 3, 2):
        spread_wait(vpa, 24, k)
        spread_wait(vpa, 24, k + 4)
    right = gr[:, :, :, :, :, 640:1280].reshape(1024, 640)
    for a in range(0, 320, 64):
        vu_ref[a : a + 64] = outer(vpa[a : a + 64], right)

    for c in pending:
        c.wait_send()
    for k in range(1, 8):
        for h in (0, 1):
            key_copy(k, h).wait_send()
    for b in range(8):
        copy(psend.at[b], rsib.at[b], s_core.at[b], r_core.at[b], c_dev).wait_send()
        copy(ysend.at[b], ry.at[b], s_y.at[b], r_y.at[b], y_dev).wait_send()
    vd_add(5, 6, 7)
    vd = SIGMA * jnp.sum(jnp.where(spot, vdt[pl.ds(st, 1)], 0.0), axis=1, keepdims=True)
    for c, w in enumerate(spans):
        total = gathered(0, w) + rn2[0, 0, :, w].astype(F32) + rn2[1, 0, :, w].astype(F32)
        total = total + vd * vsv[:, w].astype(F32)
        for k in (0, 1, 2):
            _, dst, ssem, rsem, dev = far_copy(k, c)
            arrive(dst, ssem, rsem, dev)
            total = total + rf[k, :, w].astype(F32)
        out_ref[:, w] = total.astype(BF)


def store(*refs):
    copies = [pltpu.make_async_copy(a, b, refs[6].at[k]) for k, (a, b) in enumerate(zip(refs[0:3], refs[3:6]))]
    for c in copies:
        c.start()
    for c in copies:
        c.wait()


def body(*args):
    x, kw, vw, kp, ks, vp, vs, fitness = args
    vm = pl.BlockSpec(memory_space=pltpu.VMEM)
    dma = pltpu.SemaphoreType.DMA
    args = (pltpu.with_memory_space_constraint(a, pltpu.HBM) for a in (x, kw.T, vw, kp, ks.T, vp.T, vs, fitness.reshape(1, 16)))
    out, ku, vu = pl.pallas_call(
        kernel,
        out_shape=(
            jax.ShapeDtypeStruct((16, 640), BF),
            jax.ShapeDtypeStruct((320, 640), BF),
            jax.ShapeDtypeStruct((320, 640), BF),
        ),
        in_specs=[pl.BlockSpec(memory_space=pltpu.HBM)] * 8,
        out_specs=(vm, vm, vm),
        scratch_shapes=[
            pltpu.VMEM((320, 640), BF),
            pltpu.VMEM((320, 640), BF),
            pltpu.VMEM((1, 16), BF),
            pltpu.VMEM((16, 640), BF),
            pltpu.VMEM((8, 2, 2, 2, 16, 640), BF),
            pltpu.VMEM((8, 2, 2, 2, 16, 1280), BF),
            pltpu.VMEM((8, 320, 128), BF),
            pltpu.VMEM((320, 1024), BF),
            pltpu.VMEM((8, 320, 128), BF),
            pltpu.VMEM((8, 320, 128), BF),
            pltpu.VMEM((8, 336, 128), BF),
            pltpu.VMEM((320, 1024), BF),
            pltpu.VMEM((8, 2, 2, 2, 16, 640), F32),
            pltpu.VMEM((8, 2, 2, 16, 640), BF),
            pltpu.VMEM((8, 2, 2, 16, 640), BF),
            pltpu.VMEM((8, 2, 16, 640), BF),
            pltpu.VMEM((8, 2, 16, 640), BF),
            pltpu.VMEM((8, 2, 16, 640), F32),
            pltpu.VMEM((8, 2, 16, 640), BF),
            pltpu.VMEM((2, 4, 16, 640), BF),
            pltpu.VMEM((2, 2, 16, 640), BF),
            pltpu.VMEM((3, 16, 640), BF),
            pltpu.VMEM((3, 16, 640), BF),
            pltpu.VMEM((8, 128), F32),
            pltpu.VMEM((4, 8, 128), F32),
            pltpu.VMEM((8, 8, 128), F32),
            pltpu.VMEM((16, 128), F32),
            pltpu.VMEM((4, 16, 128), F32),
            pltpu.VMEM((8, 16, 128), F32),
        ]
        + [dma((n,)) for n in (8, 15, 15, 16, 16, 8, 8, 32, 32)]
        + [dma(()), dma(())]
        + [dma((n,)) for n in (34, 34, 48, 48, 8, 8, 8, 8, 12, 12, 6, 6, 8, 8, 8, 8)],
        compiler_params=pltpu.CompilerParams(
            collective_id=0, has_side_effects=True, vmem_limit_bytes=48 * 2**20
        ),
        cost_estimate=pl.CostEstimate(flops=1_700_000_000, bytes_accessed=4_000_000, transcendentals=0),
        name="step",
    )(*args)
    anywhere = pl.BlockSpec(memory_space=pl.ANY)
    out, ku, vu = pl.pallas_call(
        store,
        out_shape=tuple(jax.ShapeDtypeStruct(a.shape, BF) for a in (out, ku, vu)),
        in_specs=[anywhere] * 3,
        out_specs=(anywhere,) * 3,
        scratch_shapes=[dma((3,))],
        compiler_params=pltpu.CompilerParams(vmem_limit_bytes=2 * 2**20),
        name="store",
    )(out, ku, vu)
    return out, ku.T, vu


def solution(mesh):
    placed = (
        P("member", "tensor"), P("tensor", "member"), P("member", "tensor"), P("member", "tensor"),
        P("tensor", "member"), P("tensor", "member"), P("member", "tensor"), P("member"),
    )
    return jax.shard_map(
        body,
        mesh=mesh,
        in_specs=placed,
        out_specs=(P("member", "tensor"), P("tensor", "member"), P("member", "tensor")),
        check_vma=False,
    )
```

```python
import functools

import jax
import jax.numpy as jnp
from jax import lax
from jax.experimental import pallas as pl
from jax.experimental.pallas import tpu as pltpu
from jax.sharding import PartitionSpec as P

BF, F32 = jnp.bfloat16, jnp.float32
MESH = pl.DeviceIdType.MESH
SIGMA = 0.005

FAR = (4, -4, 8)
NEAR = (
    (1, 0), (-1, 0), (2, 0), (-2, 0),
    (1, -4), (-1, -4), (2, -4),
    (1, 4), (-1, 4), (-2, 4),
    (1, 8), (-1, 8),
)
OFFSETS = (0, -1, 1, -2, 2, -4, 4, -5, 3, -3, 5, -6, 6, 8, 7, -7)


def kernel(
    x_ref, kw_ref, vw_ref, kp_ref, ks_ref, vp_ref, vs_ref, f_ref,
    out_ref, ku_ref, vu_ref,
    kw, vw, fv, vsv, gi, gr, ksa, vpa, bsend, rsb, hid, wgt_k, pbuf, psend, rsib, ysend, ry, zf, zb, rn, rn2, fb, rf, vdt, vds, vdr, mt, mts, mtr,
    ls, ss, rr, gv, tr, r_core, r_y,
):
    m, t = lax.axis_index("member"), lax.axis_index("tensor")
    z, half, core = m // 4, (m // 2) % 2, m % 2
    other, sib = 1 - half, 1 - core

    def at_z(dz):
        return (lax.rem(z + dz + 16, 16) * 4 + half * 2 + core, t)

    y_dev = (z * 4 + other * 2 + core, t)
    c_dev = (z * 4 + half * 2 + sib, t)

    def tau(tt):
        return lax.rem(tt, 2) * 4 + tt // 2

    def slot(dz):
        zz = lax.rem(z + dz + 16, 16)
        return (lax.rem(zz, 4) // 2) * 4 + zz // 4, lax.rem(zz, 2)

    def klass(r):
        cc = lax.rem(z + r, 4)
        return pl.ds((cc // 2) * 4, 4), lax.rem(cc, 2)

    def cols(tt):
        return pl.ds(pl.multiple_of(tt * 128, 128), 128)

    parts = (pl.ds(0, 160), pl.ds(160, 176))

    def at_block(buf, tt, part=None):
        if buf is vpa:
            return buf.at[:, cols(tt)]
        return buf.at[tt] if part is None else buf.at[tt, parts[part]]

    me_tau = tau(t)

    class Shared:
        def __init__(self, ref, which):
            self.ref, self.which, self.at = ref, which, self

        def __getitem__(self, k):
            return self.ref.at[self.which(k) if callable(self.which) else self.which]

    zs = Shared(ss, lambda k: 0 if k < 7 else 1)
    ys, cs, cs2, s_ks, s_vp, s_key, s_core, s_y, s_mt, s_vd = (Shared(ss, n) for n in range(2, 12))
    gs = Shared(ss, lambda k: 12 if k in (14, 31) else 13)
    s_hid = Shared(ss, lambda k: 14 + k // 8)
    s_z = Shared(ss, lambda k: 16 + k // 6)
    s_f = Shared(ss, lambda k: 18 + k // 3)
    ys2, yr2 = ss.at[20], rr.at[0]
    zr = Shared(rr, lambda k: 1 + k if k < 3 else 4 if k < 7 else 5 if k < 13 else 6)
    yr = Shared(rr, lambda k: 7 + OFFSETS[k] % 4)
    cr, cr2 = Shared(rr, 11), Shared(rr, 12)
    r_ks = Shared(rr, lambda k: 13 if k == 4 else 14)
    r_vp = Shared(rr, lambda k: 15 if k == 4 else 16)
    r_key = Shared(rr, lambda h: 17 + h)
    r_z = Shared(rr, lambda k: 19 + 2 * (k // 6) + (0 if k % 6 < 2 else 1))
    r_f = Shared(rr, lambda k: 23 + k // 3)
    tiles = lambda k: k if k < 2 else 2 if k < 5 else 3
    r_vd = Shared(rr, lambda k: 25 + tiles(k))
    r_mt = Shared(tr, lambda k: 16 + tiles(k))

    def copy(src, dst, ssem, rsem, dev):
        return pltpu.make_async_remote_copy(
            src_ref=src, dst_ref=dst, send_sem=ssem, recv_sem=rsem, device_id=dev, device_id_type=MESH
        )

    def send(src, dst, ssem, rsem, dev):
        copy(src, dst, ssem, rsem, dev).start()

    def sent(ref, sem):
        copy(ref, ref, sem, sem, c_dev).wait_send()

    def arrive(dst, ssem, rsem, dev):
        copy(dst, dst, ssem, rsem, dev).wait_recv()

    bar = pltpu.get_barrier_semaphore()
    partners = [at_z(d) for d in (8, 4, -4, 1, -1, 2, -2)] + [y_dev, c_dev]
    partners += [(m, lax.rem(t + k, 8)) for k in range(1, 8)]
    for dev in partners:
        pl.semaphore_signal(bar, inc=1, device_id=dev, device_id_type=MESH)

    def chunk(g, dz, hh=None, cc=None):
        a, b = slot(dz)
        return g.at[a, b, half if hh is None else hh, core if cc is None else cc]

    def block(g, r, hh, cc):
        a, b = klass(r)
        return g.at[a, b, hh, cc]

    st, sl = slot(0)
    mine_i, mine_r = gi.at[st, sl, half, core], gr.at[st, sl, half, core]
    loads = [
        pltpu.make_async_copy(src, dst, ls.at[k])
        for k, (src, dst) in enumerate(
            (
                (x_ref, mine_i), (kp_ref, mine_r.at[:, 0:640]), (vs_ref, vsv),
                (ks_ref, ksa.at[me_tau]), (vp_ref, vpa.at[:, cols(me_tau)]), (f_ref, fv), (kw_ref, kw), (vw_ref, vw),
            )
        )
    ]
    for c in loads:
        c.start()

    first = sl * 64 + half * 32 + core * 16
    spot = lax.broadcasted_iota(jnp.int32, (16, 128), 1) == first + lax.broadcasted_iota(jnp.int32, (16, 128), 0)

    def place(col):
        return jnp.sum(jnp.where(spot, col, 0.0), axis=0, keepdims=True)

    mt[...] = jnp.zeros((16, 128), F32)
    for c in loads[0:6]:
        c.wait()
    fit = jnp.broadcast_to(fv[...].astype(F32), (16, 16))
    row, lane = (lax.broadcasted_iota(jnp.int32, (16, 16), d) for d in (0, 1))
    fit = jnp.sum(jnp.where(row == lane, fit, 0.0), axis=1, keepdims=True) * (1.0 / 32.0)
    dots = jnp.sum(mine_i[...].astype(F32) * mine_r[:, 0:640].astype(F32), axis=1, keepdims=True)
    mt[pl.ds(st, 1)] = place(dots * SIGMA)
    mt[pl.ds(8 + st, 1)] = place(fit)
    mine_r[:, 640:1280] = (fit * vsv[...].astype(F32)).astype(BF)

    pl.semaphore_wait(bar, len(partners))

    def near_send(o):
        for k, (d, oo) in enumerate(NEAR):
            if oo == o:
                send(chunk(gi, o), chunk(gi, o), zs.at[3 + k], zr.at[3 + k], at_z(d))

    def far_wait(k):
        arrive(chunk(gi, -FAR[k]), zs.at[k], zr.at[k], at_z(-FAR[k]))

    def near_wait(*os):
        came = [(k, oo - d) for k, (d, oo) in enumerate(NEAR) if oo in os]
        k = 3 + came[0][0]
        arrive(gi.at[pl.ds(0, len(came)), 0, 0, 0], zs.at[k], zr.at[k], c_dev)
        for _, dz in came:
            y_send(dz)

    def y_send(dz):
        dz = dz if dz <= 8 else dz - 16
        k = OFFSETS.index(dz)
        send(chunk(gi, dz), chunk(gi, dz), ys.at[k], yr.at[k], y_dev)

    ty = lax.rem(t + 4, 8)

    def along_x(k):
        return (t // 4) * 4 + lax.rem(t + k, 4)

    def source(k):
        return lax.rem((t // 4) * 4 + lax.rem(t + 4 - lax.rem(k, 4), 4) + 4 * (k // 4), 8)

    def spread_sems(buf, base):
        if buf is ksa:
            return s_ks, r_ks
        return (s_vp, r_vp) if buf is vpa else (Shared(ss, 14 + base // 8), tr)

    def spread_copy(buf, base, part, k, frm, to):
        b = at_block(buf, tau(frm), part)
        ssem, rsem = spread_sems(buf, base)
        i = base + k
        send(b, b, ssem.at[i], rsem.at[i], (m, to))

    def spread(buf, base, part=None):
        for k, to in ((4, ty), (2, along_x(2)), (1, along_x(1)), (3, along_x(3))):
            spread_copy(buf, base, part, k, t, to)

    def pass_on(buf, base, part=None, to=(2, 1, 3)):
        spread_wait(buf, base, 4, part)
        for k in to:
            spread_copy(buf, base, part, 4 + k, ty, along_x(k))

    def pass_back(buf, base, part):
        spread_wait(buf, base, 2, part)
        spread_copy(buf, base, part, 6, along_x(2), ty)

    def spread_wait(buf, base, k, part=None):
        ssem, rsem = spread_sems(buf, base)
        i = base + k
        arrive(at_block(buf, tau(source(k)), part), ssem.at[i], rsem.at[i], (m, ty))

    def ring_send(s):
        for hh in (0, 1):
            for sign in (1, -1):
                if s == 8 and (hh == 0) != (sign > 0):
                    continue
                i = (sign < 0) * 16 + (s - 1) * 2 + hh
                c = chunk(gr, -sign * (s - 1), hh)
                send(c, c, gs.at[i], gv.at[i], at_z(sign))

    def ring_wait(s):
        for hh in (0, 1):
            for sign in (1, -1):
                if s == 8 and (hh == 0) != (sign > 0):
                    continue
                i = (sign < 0) * 16 + (s - 1) * 2 + hh
                c = chunk(gr, -sign * s, hh)
                arrive(c, gs.at[i], gv.at[i], at_z(-sign))
                if s < 7 or (s == 7 and (hh == 0) == (sign > 0)):
                    n = i + 2
                    send(c, c, gs.at[n], gv.at[n], at_z(sign))
                send(c, c, cs2.at[i], cr2.at[i], c_dev)

    def ring_end():
        arrive(gr.at[pl.ds(0, 4)], cs2.at[0], cr2.at[0], c_dev)

    def round_of(tile, held, got, ssem, rsem):
        def begin(n, *links):
            held[n] = tile[...]
            for k, dev in links:
                send(held.at[n], got.at[k], ssem.at[k], rsem.at[k], dev)

        def end(*ks):
            arrive(got.at[pl.ds(ks[0], len(ks))], ssem.at[ks[0]], rsem.at[ks[0]], c_dev)
            for k in ks:
                tile[...] += got[k]

        return begin, end

    mt_send, mt_add = round_of(mt, mts, mtr, s_mt, r_mt)
    vd_send, vd_add = round_of(vdt, vds, vdr, s_vd, r_vd)
    near_links = ((2, at_z(1)), (3, at_z(-1)), (4, at_z(-2)))
    far_links = ((5, at_z(4)), (6, at_z(-4)), (7, at_z(8)))

    mt_send(0, *far_links)
    for k in (2, 0, 1):
        send(chunk(gi, 0), chunk(gi, 0), zs.at[k], zr.at[k], at_z(FAR[k]))
    near_send(0)
    y_send(0)
    send(mine_r, mine_r, ys2, yr2, y_dev)
    spread(ksa, 0)

    for k, o in ((0, -4), (1, 4)):
        far_wait(k)
        near_send(o)
    near_wait(0)
    for o in (-4, 4):
        y_send(o)
    far_wait(2)
    near_send(8)
    y_send(8)
    mt_add(5, 6, 7)
    mt_send(1, *near_links)
    theirs = chunk(gr, 0, other)
    arrive(theirs, ys2, yr2, y_dev)
    ring_send(1)
    for hh in (0, 1):
        c = chunk(gr, 0, hh)
        send(c, c, cs2.at[32 + hh], cr2.at[32 + hh], c_dev)
    pass_on(ksa, 0)
    near_wait(-4, 4)
    near_wait(8)
    mt_add(2, 3, 4)
    mt_send(2, (1, y_dev))
    for r in range(4):
        send(block(gi, r, half, core), block(gi, r, half, core), cs.at[r], cr.at[r], c_dev)
    ring_wait(1)
    for r in range(4):
        arrive(block(gi, r, other, core), ys.at[r], rr.at[7 + r], y_dev)
        send(block(gi, r, other, core), block(gi, r, other, core), cs.at[4 + r], cr.at[4 + r], c_dev)
    mt_add(1)
    mt_send(3, (0, c_dev))
    arrive(ksa.at[pl.ds(0, 6)], s_ks.at[0], r_ks.at[0], c_dev)
    for c in loads[6:]:
        c.wait()
    arrive(gi.at[pl.ds(0, 4)], cs.at[0], cr.at[0], c_dev)

    mt_add(0)
    ring_wait(2)
    def key_block(tt):
        rows = gi[tt].reshape(128, 640)
        dp = mt[pl.ds(tt, 1)]
        part = lax.dot_general(
            kw[...], rows, (((1,), (1,)), ((), ())), preferred_element_type=F32
        )
        return (part + dp * ksa[tt].astype(F32)).astype(BF)

    def key_copy(k, h):
        tgt = lax.rem(t + k, 8)
        u = pl.ds(h * 160, 160)
        return copy(bsend.at[k, u], rsb.at[me_tau, u], s_key.at[0], rr.at[17 + h], (m, tgt))

    def key_step(i, carry):
        k = 7 - i
        bsend[k] = key_block(tau(lax.rem(t + k, 8)))
        key_copy(k, 0).start()
        return carry

    lax.fori_loop(0, 7, key_step, 0)
    for k in range(7, 0, -1):
        key_copy(k, 1).start()
    rsb[me_tau] = key_block(me_tau)

    def weigh_k(b, carry):
        wgt_k[:, cols(b)] = (mt[pl.ds(8 + b, 1)] * ksa[b].astype(F32)).astype(BF)
        return carry

    lax.fori_loop(0, 8, weigh_k, 0)
    ring_wait(3)
    def value_step(p, k):
        b = tau(source(k))
        tail = hid[b, 320:336].astype(F32)
        vdt[pl.ds(b, 1)] = tail[0:1] + tail[1:2]
        part = lax.dot_general(
            hid[b, 0:320], vw[...], (((0,), (0,)), ((), ())), preferred_element_type=F32
        )
        pbuf[p] = part.reshape(2, 2, 2, 16, 640)
        psend[p] = pbuf[p, :, :, sib].astype(BF)
        copy(psend.at[p], rsib.at[p], s_core.at[p], r_core.at[p], c_dev).start()

    def y_step(p):
        arrive(rsib.at[p], s_core.at[p], r_core.at[p], c_dev)
        ysend[p] = (pbuf[p, :, other, core] + rsib[p, :, other].astype(F32)).astype(BF)
        copy(ysend.at[p], ry.at[p], s_y.at[p], r_y.at[p], y_dev).start()

    def z_step(p, k):
        b = tau(source(k))
        arrive(ry.at[p], s_y.at[p], r_y.at[p], y_dev)
        total = pbuf[p, :, half, core] + rsib[p, :, half].astype(F32) + ry[p].astype(F32)
        zf[b] = total
        zb[b] = total.astype(BF)

    vd = jnp.zeros((1, 128), F32)
    for h in (0, 1):
        u = pl.ds(h * 160, 160)
        arrive(rsb.at[pl.ds(0, 7), u], s_key.at[0], rr.at[17 + h], c_dev)
        pre = rsb[0, u].astype(F32)
        for k in range(1, 8):
            pre = pre + rsb[k, u].astype(F32)
        act = jnp.maximum(pre, 0.0)
        act = (act * act).astype(BF)
        hid[me_tau, u] = act
        vd = vd + jnp.sum(act.astype(F32) * vpa[u, cols(me_tau)].astype(F32), axis=0, keepdims=True)
        if h == 1:
            vhigh = vd.astype(BF).astype(F32)
            line = lax.broadcasted_iota(jnp.int32, (16, 128), 0)
            tail = jnp.where(line == 0, vhigh, jnp.where(line == 1, vd - vhigh, 0.0))
            hid[me_tau, 320:336] = tail.astype(BF)
        spread(hid, 8 * h, h)
        if h == 0:
            ring_wait(4)
    pass_on(hid, 0, 0, (1, 3))
    value_step(0, 0)
    ring_wait(5)
    pass_on(hid, 8, 1, (1, 3))
    pass_back(hid, 0, 0)
    value_step(1, 4)
    y_step(0)
    pass_back(hid, 8, 1)
    value_step(2, 2)
    y_step(1)

    def value_loop(p, carry):
        k = 2 * p - 5
        spread_wait(hid, 0, k, 0)
        spread_wait(hid, 8, k, 1)
        value_step(p, k)
        y_step(p - 1)
        return carry

    lax.fori_loop(3, 5, value_loop, 0)
    ring_wait(6)
    lax.fori_loop(5, 7, value_loop, 0)
    spread_wait(hid, 0, 6, 0)
    spread_wait(hid, 8, 6, 1)
    value_step(7, 6)
    y_step(6)
    vd_send(0, (0, c_dev))
    y_step(7)
    vd_add(0)
    vd_send(1, (1, y_dev))
    spread(vpa, 0)
    ring_wait(7)
    z_step(0, 0)
    z_step(1, 4)
    z_step(2, 2)

    def z_loop(p, carry):
        z_step(p, 2 * p - 5)
        return carry

    lax.fori_loop(3, 5, z_loop, 0)
    ring_wait(8)
    lax.fori_loop(5, 7, z_loop, 0)
    z_step(7, 6)

    spans = (pl.ds(0, 384), pl.ds(384, 256))

    def near_copies(c):
        w = spans[c]
        out = []
        for k, d in enumerate((1, -1)):
            a, b = klass(d + 4)
            out.append((zb.at[a, b, :, w], rn.at[k, :, :, w], d))
        for k, d in enumerate((2, -2)):
            for j, v in enumerate((d, 3 * d)):
                a, b = slot(v)
                out.append((zb.at[a, b, :, w], rn2.at[k, j, :, w], d))
        return out

    for c in (0, 1):
        for i, (src, dst, d) in enumerate(near_copies(c)):
            send(src, dst, s_z.at[6 * c + i], r_z.at[6 * c + i], at_z(d))
    vd_add(1)
    vd_send(2, *near_links)
    pass_on(vpa, 0)

    def gathered(dz, w):
        a, b = slot(dz)
        za = lax.rem(a, 4)
        return zf[a, b, :, w] + rn[0, za, :, w].astype(F32) + rn[1, za, :, w].astype(F32)

    def far_copy(k, c):
        w = spans[c]
        return fb.at[k, :, w], rf.at[k, :, w], s_f.at[3 * c + k], r_f.at[3 * c + k], at_z(FAR[k])

    for c in (0, 1):
        w = spans[c]
        arrive(rn.at[:, :, :, w], s_z.at[6 * c], r_z.at[6 * c], c_dev)
        arrive(rn2.at[:, :, :, w], s_z.at[6 * c], r_z.at[6 * c + 2], c_dev)
        for k in (2, 0, 1):
            total = gathered(FAR[k], w)
            if k < 2:
                total = total + rn2[k, 1, :, w].astype(F32)
            fb[k, :, w] = total.astype(BF)
            send(*far_copy(k, c))
    vd_add(2, 3, 4)
    vd_send(3, *far_links)
    ring_end()

    def outer(left, right):
        return jnp.dot(left, right, preferred_element_type=F32).astype(BF)

    for a in range(0, 320, 64):
        ku_ref[a : a + 64] = outer(wgt_k[a : a + 64], gr[:, :, :, :, :, 0:640].reshape(1024, 640))
    arrive(vpa.at[:, pl.ds(0, 768)], s_vp.at[0], r_vp.at[0], c_dev)
    right = gr[:, :, :, :, :, 640:1280].reshape(1024, 640)
    for a in range(0, 320, 64):
        vu_ref[a : a + 64] = outer(vpa[a : a + 64], right)

    sent(gi.at[pl.ds(0, 7), 0, 0, 0], zs.at[0])
    sent(gi.at[0], zs.at[7])
    sent(gi.at[pl.ds(0, 2)], ys.at[0])
    sent(gi.at[pl.ds(0, 4)], cs.at[0])
    sent(gr.at[pl.ds(0, 7), :, :, 0], gs.at[0])
    sent(gr.at[0, 0, :, 0], gs.at[14])
    sent(gr.at[pl.ds(0, 4)], cs2.at[0])
    sent(mine_r, ys2)
    sent(ksa.at[pl.ds(0, 7)], s_ks.at[0])
    sent(vpa.at[:, pl.ds(0, 896)], s_vp.at[0])
    for h in (0, 1):
        sent(hid.at[pl.ds(0, 7), parts[h]], s_hid.at[8 * h])
    sent(bsend.at[pl.ds(1, 7)], s_key.at[0])
    sent(psend, s_core.at[0])
    sent(ysend, s_y.at[0])
    for c, w in enumerate(spans):
        sent(zb.at[pl.ds(0, 6), :, :, w], s_z.at[6 * c])
        sent(fb.at[:, :, w], s_f.at[3 * c])
    sent(mtr, s_mt.at[0])
    sent(vdr, s_vd.at[0])
    vd_add(5, 6, 7)
    vd = SIGMA * jnp.sum(jnp.where(spot, vdt[pl.ds(st, 1)], 0.0), axis=1, keepdims=True)
    for c, w in enumerate(spans):
        total = gathered(0, w) + rn2[0, 0, :, w].astype(F32) + rn2[1, 0, :, w].astype(F32)
        total = total + vd * vsv[:, w].astype(F32)
        arrive(rf.at[:, :, w], s_f.at[3 * c], r_f.at[3 * c], c_dev)
        for k in (0, 1, 2):
            total = total + rf[k, :, w].astype(F32)
        out_ref[:, w] = total.astype(BF)


def store(*refs):
    copies = [pltpu.make_async_copy(a, b, refs[6].at[k]) for k, (a, b) in enumerate(zip(refs[0:3], refs[3:6]))]
    for c in copies:
        c.start()
    for c in copies:
        c.wait()


def body(*args):
    x, kw, vw, kp, ks, vp, vs, fitness = args
    vm = pl.BlockSpec(memory_space=pltpu.VMEM)
    dma = pltpu.SemaphoreType.DMA
    args = (pltpu.with_memory_space_constraint(a, pltpu.HBM) for a in (x, kw.T, vw, kp, ks.T, vp.T, vs, fitness.reshape(1, 16)))
    out, ku, vu = pl.pallas_call(
        kernel,
        out_shape=(
            jax.ShapeDtypeStruct((16, 640), BF),
            jax.ShapeDtypeStruct((320, 640), BF),
            jax.ShapeDtypeStruct((320, 640), BF),
        ),
        in_specs=[pl.BlockSpec(memory_space=pltpu.HBM)] * 8,
        out_specs=(vm, vm, vm),
        scratch_shapes=[
            pltpu.VMEM((320, 640), BF),
            pltpu.VMEM((320, 640), BF),
            pltpu.VMEM((1, 16), BF),
            pltpu.VMEM((16, 640), BF),
            pltpu.VMEM((8, 2, 2, 2, 16, 640), BF),
            pltpu.VMEM((8, 2, 2, 2, 16, 1280), BF),
            pltpu.VMEM((8, 320, 128), BF),
            pltpu.VMEM((320, 1024), BF),
            pltpu.VMEM((8, 320, 128), BF),
            pltpu.VMEM((8, 320, 128), BF),
            pltpu.VMEM((8, 336, 128), BF),
            pltpu.VMEM((320, 1024), BF),
            pltpu.VMEM((8, 2, 2, 2, 16, 640), F32),
            pltpu.VMEM((8, 2, 2, 16, 640), BF),
            pltpu.VMEM((8, 2, 2, 16, 640), BF),
            pltpu.VMEM((8, 2, 16, 640), BF),
            pltpu.VMEM((8, 2, 16, 640), BF),
            pltpu.VMEM((8, 2, 16, 640), F32),
            pltpu.VMEM((8, 2, 16, 640), BF),
            pltpu.VMEM((2, 4, 16, 640), BF),
            pltpu.VMEM((2, 2, 16, 640), BF),
            pltpu.VMEM((3, 16, 640), BF),
            pltpu.VMEM((3, 16, 640), BF),
            pltpu.VMEM((8, 128), F32),
            pltpu.VMEM((4, 8, 128), F32),
            pltpu.VMEM((8, 8, 128), F32),
            pltpu.VMEM((16, 128), F32),
            pltpu.VMEM((4, 16, 128), F32),
            pltpu.VMEM((8, 16, 128), F32),
        ]
        + [dma((n,)) for n in (8, 21, 29, 32, 20, 8, 8)],
        compiler_params=pltpu.CompilerParams(
            collective_id=0, has_side_effects=True, vmem_limit_bytes=48 * 2**20
        ),
        cost_estimate=pl.CostEstimate(flops=1_700_000_000, bytes_accessed=4_000_000, transcendentals=0),
        name="step",
    )(*args)
    anywhere = pl.BlockSpec(memory_space=pl.ANY)
    out, ku, vu = pl.pallas_call(
        store,
        out_shape=tuple(jax.ShapeDtypeStruct(a.shape, BF) for a in (out, ku, vu)),
        in_specs=[anywhere] * 3,
        out_specs=(anywhere,) * 3,
        scratch_shapes=[dma((3,))],
        compiler_params=pltpu.CompilerParams(vmem_limit_bytes=2 * 2**20),
        name="store",
    )(out, ku, vu)
    return out, ku.T, vu


def solution(mesh):
    placed = (
        P("member", "tensor"), P("tensor", "member"), P("member", "tensor"), P("member", "tensor"),
        P("tensor", "member"), P("tensor", "member"), P("member", "tensor"), P("member"),
    )
    return jax.shard_map(
        body,
        mesh=mesh,
        in_specs=placed,
        out_specs=(P("member", "tensor"), P("tensor", "member"), P("member", "tensor")),
        check_vma=False,
    )
```

```python
import functools

import jax
import jax.numpy as jnp
from jax import lax
from jax.experimental import pallas as pl
from jax.experimental.pallas import tpu as pltpu
from jax.sharding import PartitionSpec as P

BF, F32 = jnp.bfloat16, jnp.float32
MESH = pl.DeviceIdType.MESH
SIGMA = 0.005

FAR = (4, -4, 8)
NEAR = (
    (1, 0), (-1, 0), (2, 0), (-2, 0),
    (1, -4), (-1, -4), (2, -4),
    (1, 4), (-1, 4), (-2, 4),
    (1, 8), (-1, 8),
)
OFFSETS = (0, -1, 1, -2, 2, -4, 4, -5, 3, -3, 5, -6, 6, 8, 7, -7)


def kernel(
    x_ref, kw_ref, vw_ref, kp_ref, ks_ref, vp_ref, vs_ref, f_ref,
    out_ref, ku_ref, vu_ref,
    kw, vw, fv, vsv, gi, gr, ksa, vpa, bsend, rsb, hid, wgt_k, pbuf, psend, rsib, ysend, ry, zf, zb, rn, rn2, fb, rf, vdt, vds, vdr, mt, mts, mtr,
    ls, ss, rr, gv, tr, r_core, r_y,
):
    m, t = lax.axis_index("member"), lax.axis_index("tensor")
    z, half, core = m // 4, (m // 2) % 2, m % 2
    other, sib = 1 - half, 1 - core

    def at_z(dz):
        return (lax.rem(z + dz + 16, 16) * 4 + half * 2 + core, t)

    y_dev = (z * 4 + other * 2 + core, t)
    c_dev = (z * 4 + half * 2 + sib, t)

    def tau(tt):
        return lax.rem(tt, 2) * 4 + tt // 2

    def slot(dz):
        zz = lax.rem(z + dz + 16, 16)
        return (lax.rem(zz, 4) // 2) * 4 + zz // 4, lax.rem(zz, 2)

    def klass(r):
        cc = lax.rem(z + r, 4)
        return pl.ds((cc // 2) * 4, 4), lax.rem(cc, 2)

    def cols(tt):
        return pl.ds(pl.multiple_of(tt * 128, 128), 128)

    parts = (pl.ds(0, 160), pl.ds(160, 176))

    def at_block(buf, tt, part=None):
        if buf is vpa:
            return buf.at[:, cols(tt)]
        return buf.at[tt] if part is None else buf.at[tt, parts[part]]

    me_tau = tau(t)

    class Shared:
        def __init__(self, ref, which):
            self.ref, self.which, self.at = ref, which, self

        def __getitem__(self, k):
            return self.ref.at[self.which(k) if callable(self.which) else self.which]

    zs = Shared(ss, lambda k: 0 if k < 7 else 1)
    ys, cs, cs2, s_ks, s_vp, s_key, s_core, s_y, s_mt, s_vd = (Shared(ss, n) for n in range(2, 12))
    gs = Shared(ss, lambda k: 12 if k in (14, 31) else 13)
    s_z, s_f = Shared(ss, 15), Shared(ss, 16)
    ys2, yr2 = ss.at[17], rr.at[0]
    zr = Shared(rr, lambda k: 1 + k if k < 3 else 4 if k < 7 else 5 if k < 13 else 6)
    yr = Shared(rr, lambda k: 7 + OFFSETS[k] % 4)
    cr, cr2 = Shared(rr, 11), Shared(rr, 12)
    r_ks = Shared(rr, lambda k: 13 if k == 4 else 14)
    r_vp = Shared(rr, lambda k: 15 if k == 4 else 16)
    r_key = Shared(rr, lambda h: 17 + h)
    r_z = Shared(rr, lambda k: 19 + 2 * (k // 6) + (0 if k % 6 < 2 else 1))
    r_f = Shared(rr, lambda k: 23 + k // 3)
    tiles = lambda k: k if k < 2 else 2 if k < 5 else 3
    r_vd = Shared(rr, lambda k: 25 + tiles(k))
    r_mt = Shared(tr, lambda k: 16 + tiles(k))

    def copy(src, dst, ssem, rsem, dev):
        return pltpu.make_async_remote_copy(
            src_ref=src, dst_ref=dst, send_sem=ssem, recv_sem=rsem, device_id=dev, device_id_type=MESH
        )

    def send(src, dst, ssem, rsem, dev):
        copy(src, dst, ssem, rsem, dev).start()

    def sent(ref, sem):
        copy(ref, ref, sem, sem, c_dev).wait_send()

    def arrive(dst, ssem, rsem, dev):
        copy(dst, dst, ssem, rsem, dev).wait_recv()

    bar = pltpu.get_barrier_semaphore()
    partners = [at_z(d) for d in (8, 4, -4, 1, -1, 2, -2)] + [y_dev, c_dev]
    partners += [(m, lax.rem(t + k, 8)) for k in range(1, 8)]
    for dev in partners:
        pl.semaphore_signal(bar, inc=1, device_id=dev, device_id_type=MESH)

    def chunk(g, dz, hh=None, cc=None):
        a, b = slot(dz)
        return g.at[a, b, half if hh is None else hh, core if cc is None else cc]

    def block(g, r, hh, cc):
        a, b = klass(r)
        return g.at[a, b, hh, cc]

    st, sl = slot(0)
    mine_i, mine_r = gi.at[st, sl, half, core], gr.at[st, sl, half, core]
    loads = [
        pltpu.make_async_copy(src, dst, ls.at[k])
        for k, (src, dst) in enumerate(
            (
                (x_ref, mine_i), (kp_ref, mine_r.at[:, 0:640]), (vs_ref, vsv),
                (ks_ref, ksa.at[me_tau]), (vp_ref, vpa.at[:, cols(me_tau)]), (f_ref, fv), (kw_ref, kw), (vw_ref, vw),
            )
        )
    ]
    for c in loads:
        c.start()

    first = sl * 64 + half * 32 + core * 16
    spot = lax.broadcasted_iota(jnp.int32, (16, 128), 1) == first + lax.broadcasted_iota(jnp.int32, (16, 128), 0)

    def place(col):
        return jnp.sum(jnp.where(spot, col, 0.0), axis=0, keepdims=True)

    mt[...] = jnp.zeros((16, 128), F32)
    for c in loads[0:6]:
        c.wait()
    fit = jnp.broadcast_to(fv[...].astype(F32), (16, 16))
    row, lane = (lax.broadcasted_iota(jnp.int32, (16, 16), d) for d in (0, 1))
    fit = jnp.sum(jnp.where(row == lane, fit, 0.0), axis=1, keepdims=True) * (1.0 / 32.0)
    dots = jnp.sum(mine_i[...].astype(F32) * mine_r[:, 0:640].astype(F32), axis=1, keepdims=True)
    mt[pl.ds(st, 1)] = place(dots * SIGMA)
    mt[pl.ds(8 + st, 1)] = place(fit)
    mine_r[:, 640:1280] = (fit * vsv[...].astype(F32)).astype(BF)

    pl.semaphore_wait(bar, len(partners))

    def near_send(o):
        for k, (d, oo) in enumerate(NEAR):
            if oo == o:
                send(chunk(gi, o), chunk(gi, o), zs.at[3 + k], zr.at[3 + k], at_z(d))

    def far_wait(k):
        arrive(chunk(gi, -FAR[k]), zs.at[k], zr.at[k], at_z(-FAR[k]))

    def near_wait(*os):
        came = [(k, oo - d) for k, (d, oo) in enumerate(NEAR) if oo in os]
        k = 3 + came[0][0]
        arrive(gi.at[pl.ds(0, len(came)), 0, 0, 0], zs.at[k], zr.at[k], c_dev)
        for _, dz in came:
            y_send(dz)

    def y_send(dz):
        dz = dz if dz <= 8 else dz - 16
        k = OFFSETS.index(dz)
        send(chunk(gi, dz), chunk(gi, dz), ys.at[k], yr.at[k], y_dev)

    ty = lax.rem(t + 4, 8)

    def along_x(k):
        return (t // 4) * 4 + lax.rem(t + k, 4)

    def source(k):
        return lax.rem((t // 4) * 4 + lax.rem(t + 4 - lax.rem(k, 4), 4) + 4 * (k // 4), 8)

    def spread_sems(buf, base):
        if buf is ksa:
            return s_ks, r_ks
        return (s_vp, r_vp) if buf is vpa else (Shared(ss, 14), tr)

    def spread_copy(buf, base, part, k, frm, to):
        b = at_block(buf, tau(frm), part)
        ssem, rsem = spread_sems(buf, base)
        i = base + k
        send(b, b, ssem.at[i], rsem.at[i], (m, to))

    def spread(buf, base, part=None):
        for k, to in ((4, ty), (2, along_x(2)), (1, along_x(1)), (3, along_x(3))):
            spread_copy(buf, base, part, k, t, to)

    def pass_on(buf, base, part=None, to=(2, 1, 3)):
        spread_wait(buf, base, 4, part)
        for k in to:
            spread_copy(buf, base, part, 4 + k, ty, along_x(k))

    def pass_back(buf, base, part):
        spread_wait(buf, base, 2, part)
        spread_copy(buf, base, part, 6, along_x(2), ty)

    def spread_wait(buf, base, k, part=None):
        ssem, rsem = spread_sems(buf, base)
        i = base + k
        arrive(at_block(buf, tau(source(k)), part), ssem.at[i], rsem.at[i], (m, ty))

    def ring_send(s):
        for hh in (0, 1):
            for sign in (1, -1):
                if s == 8 and (hh == 0) != (sign > 0):
                    continue
                i = (sign < 0) * 16 + (s - 1) * 2 + hh
                c = chunk(gr, -sign * (s - 1), hh)
                send(c, c, gs.at[i], gv.at[(s - 1) * 2 + hh], at_z(sign))

    def ring_wait(s):
        for hh in (0, 1):
            signs = (1, -1) if s < 8 else ((1,) if hh == 0 else (-1,))
            n = (s - 1) * 2 + hh
            arrive(gr.at[0, 0, pl.ds(0, len(signs)), 0], gs.at[0], gv.at[n], c_dev)
            for sign in signs:
                i = (sign < 0) * 16 + n
                c = chunk(gr, -sign * s, hh)
                if s < 7 or (s == 7 and (hh == 0) == (sign > 0)):
                    send(c, c, gs.at[i + 2], gv.at[n + 2], at_z(sign))
                send(c, c, cs2.at[i], cr2.at[i], c_dev)

    def ring_end():
        arrive(gr.at[pl.ds(0, 4)], cs2.at[0], cr2.at[0], c_dev)

    def round_of(tile, held, got, ssem, rsem):
        def begin(n, *links):
            held[n] = tile[...]
            for k, dev in links:
                send(held.at[n], got.at[k], ssem.at[k], rsem.at[k], dev)

        def end(*ks):
            arrive(got.at[pl.ds(ks[0], len(ks))], ssem.at[ks[0]], rsem.at[ks[0]], c_dev)
            for k in ks:
                tile[...] += got[k]

        return begin, end

    mt_send, mt_add = round_of(mt, mts, mtr, s_mt, r_mt)
    vd_send, vd_add = round_of(vdt, vds, vdr, s_vd, r_vd)
    near_links = ((2, at_z(1)), (3, at_z(-1)), (4, at_z(-2)))
    far_links = ((5, at_z(4)), (6, at_z(-4)), (7, at_z(8)))

    mt_send(0, *far_links)
    for k in (2, 0, 1):
        send(chunk(gi, 0), chunk(gi, 0), zs.at[k], zr.at[k], at_z(FAR[k]))
    near_send(0)
    y_send(0)
    send(mine_r, mine_r, ys2, yr2, y_dev)
    spread(ksa, 0)

    for k, o in ((0, -4), (1, 4)):
        far_wait(k)
        near_send(o)
    near_wait(0)
    for o in (-4, 4):
        y_send(o)
    far_wait(2)
    near_send(8)
    y_send(8)
    mt_add(5, 6, 7)
    mt_send(1, *near_links)
    theirs = chunk(gr, 0, other)
    arrive(theirs, ys2, yr2, y_dev)
    ring_send(1)
    for hh in (0, 1):
        c = chunk(gr, 0, hh)
        send(c, c, cs2.at[32 + hh], cr2.at[32 + hh], c_dev)
    pass_on(ksa, 0)
    near_wait(-4, 4)
    near_wait(8)
    mt_add(2, 3, 4)
    mt_send(2, (1, y_dev))
    for r in range(4):
        send(block(gi, r, half, core), block(gi, r, half, core), cs.at[r], cr.at[r], c_dev)
    ring_wait(1)
    for r in range(4):
        arrive(block(gi, r, other, core), ys.at[r], rr.at[7 + r], y_dev)
        send(block(gi, r, other, core), block(gi, r, other, core), cs.at[4 + r], cr.at[4 + r], c_dev)
    mt_add(1)
    mt_send(3, (0, c_dev))
    arrive(ksa.at[pl.ds(0, 6)], s_ks.at[0], r_ks.at[0], c_dev)
    for c in loads[6:]:
        c.wait()
    arrive(gi.at[pl.ds(0, 4)], cs.at[0], cr.at[0], c_dev)

    mt_add(0)
    ring_wait(2)
    def key_block(tt):
        rows = gi[tt].reshape(128, 640)
        dp = mt[pl.ds(tt, 1)]
        part = lax.dot_general(
            kw[...], rows, (((1,), (1,)), ((), ())), preferred_element_type=F32
        )
        return (part + dp * ksa[tt].astype(F32)).astype(BF)

    def key_copy(k, h):
        tgt = lax.rem(t + k, 8)
        u = pl.ds(h * 160, 160)
        return copy(bsend.at[k, u], rsb.at[me_tau, u], s_key.at[0], rr.at[17 + h], (m, tgt))

    def key_step(i, carry):
        k = 7 - i
        bsend[k] = key_block(tau(lax.rem(t + k, 8)))
        key_copy(k, 0).start()
        return carry

    lax.fori_loop(0, 7, key_step, 0)
    for k in range(7, 0, -1):
        key_copy(k, 1).start()
    rsb[me_tau] = key_block(me_tau)

    def weigh_k(b, carry):
        wgt_k[:, cols(b)] = (mt[pl.ds(8 + b, 1)] * ksa[b].astype(F32)).astype(BF)
        return carry

    lax.fori_loop(0, 8, weigh_k, 0)
    ring_wait(3)
    def value_step(p, k):
        b = tau(source(k))
        tail = hid[b, 320:336].astype(F32)
        vdt[pl.ds(b, 1)] = tail[0:1] + tail[1:2]
        part = lax.dot_general(
            hid[b, 0:320], vw[...], (((0,), (0,)), ((), ())), preferred_element_type=F32
        )
        pbuf[p] = part.reshape(2, 2, 2, 16, 640)
        psend[p] = pbuf[p, :, :, sib].astype(BF)
        copy(psend.at[p], rsib.at[p], s_core.at[p], r_core.at[p], c_dev).start()

    def y_step(p):
        arrive(rsib.at[p], s_core.at[p], r_core.at[p], c_dev)
        ysend[p] = (pbuf[p, :, other, core] + rsib[p, :, other].astype(F32)).astype(BF)
        copy(ysend.at[p], ry.at[p], s_y.at[p], r_y.at[p], y_dev).start()

    def z_step(p, k):
        b = tau(source(k))
        arrive(ry.at[p], s_y.at[p], r_y.at[p], y_dev)
        total = pbuf[p, :, half, core] + rsib[p, :, half].astype(F32) + ry[p].astype(F32)
        zf[b] = total
        zb[b] = total.astype(BF)

    vd = jnp.zeros((1, 128), F32)
    for h in (0, 1):
        u = pl.ds(h * 160, 160)
        arrive(rsb.at[pl.ds(0, 7), u], s_key.at[0], rr.at[17 + h], c_dev)
        pre = rsb[0, u].astype(F32)
        for k in range(1, 8):
            pre = pre + rsb[k, u].astype(F32)
        act = jnp.maximum(pre, 0.0)
        act = (act * act).astype(BF)
        hid[me_tau, u] = act
        vd = vd + jnp.sum(act.astype(F32) * vpa[u, cols(me_tau)].astype(F32), axis=0, keepdims=True)
        if h == 1:
            vhigh = vd.astype(BF).astype(F32)
            line = lax.broadcasted_iota(jnp.int32, (16, 128), 0)
            tail = jnp.where(line == 0, vhigh, jnp.where(line == 1, vd - vhigh, 0.0))
            hid[me_tau, 320:336] = tail.astype(BF)
        spread(hid, 8 * h, h)
        if h == 0:
            ring_wait(4)
    pass_on(hid, 0, 0, (1, 3))
    value_step(0, 0)
    ring_wait(5)
    pass_on(hid, 8, 1, (1, 3))
    pass_back(hid, 0, 0)
    value_step(1, 4)
    y_step(0)
    pass_back(hid, 8, 1)
    value_step(2, 2)
    y_step(1)

    def value_loop(p, carry):
        k = 2 * p - 5
        spread_wait(hid, 0, k, 0)
        spread_wait(hid, 8, k, 1)
        value_step(p, k)
        y_step(p - 1)
        return carry

    lax.fori_loop(3, 5, value_loop, 0)
    ring_wait(6)
    lax.fori_loop(5, 7, value_loop, 0)
    spread_wait(hid, 0, 6, 0)
    spread_wait(hid, 8, 6, 1)
    value_step(7, 6)
    y_step(6)
    vd_send(0, (0, c_dev))
    y_step(7)
    vd_add(0)
    vd_send(1, (1, y_dev))
    spread(vpa, 0)
    ring_wait(7)
    z_step(0, 0)
    z_step(1, 4)
    z_step(2, 2)

    def z_loop(p, carry):
        z_step(p, 2 * p - 5)
        return carry

    lax.fori_loop(3, 5, z_loop, 0)
    ring_wait(8)
    lax.fori_loop(5, 7, z_loop, 0)
    z_step(7, 6)

    spans = (pl.ds(0, 384), pl.ds(384, 256))

    def near_copies(c):
        w = spans[c]
        out = []
        for k, d in enumerate((1, -1)):
            a, b = klass(d + 4)
            out.append((zb.at[a, b, :, w], rn.at[k, :, :, w], d))
        for k, d in enumerate((2, -2)):
            for j, v in enumerate((d, 3 * d)):
                a, b = slot(v)
                out.append((zb.at[a, b, :, w], rn2.at[k, j, :, w], d))
        return out

    for c in (0, 1):
        for i, (src, dst, d) in enumerate(near_copies(c)):
            send(src, dst, s_z.at[6 * c + i], r_z.at[6 * c + i], at_z(d))
    vd_add(1)
    vd_send(2, *near_links)
    pass_on(vpa, 0)

    def gathered(dz, w):
        a, b = slot(dz)
        za = lax.rem(a, 4)
        return zf[a, b, :, w] + rn[0, za, :, w].astype(F32) + rn[1, za, :, w].astype(F32)

    def far_copy(k, c):
        w = spans[c]
        return fb.at[k, :, w], rf.at[k, :, w], s_f.at[3 * c + k], r_f.at[3 * c + k], at_z(FAR[k])

    for c in (0, 1):
        w = spans[c]
        arrive(rn.at[:, :, :, w], s_z.at[6 * c], r_z.at[6 * c], c_dev)
        arrive(rn2.at[:, :, :, w], s_z.at[6 * c], r_z.at[6 * c + 2], c_dev)
        for k in (2, 0, 1):
            total = gathered(FAR[k], w)
            if k < 2:
                total = total + rn2[k, 1, :, w].astype(F32)
            fb[k, :, w] = total.astype(BF)
            send(*far_copy(k, c))
    vd_add(2, 3, 4)
    vd_send(3, *far_links)
    ring_end()

    def outer(left, right):
        return jnp.dot(left, right, preferred_element_type=F32).astype(BF)

    for a in range(0, 320, 64):
        ku_ref[a : a + 64] = outer(wgt_k[a : a + 64], gr[:, :, :, :, :, 0:640].reshape(1024, 640))
    arrive(vpa.at[:, pl.ds(0, 768)], s_vp.at[0], r_vp.at[0], c_dev)
    right = gr[:, :, :, :, :, 640:1280].reshape(1024, 640)
    for a in range(0, 320, 64):
        vu_ref[a : a + 64] = outer(vpa[a : a + 64], right)

    sent(gi.at[pl.ds(0, 7), 0, 0, 0], zs.at[0])
    sent(gi.at[0], zs.at[7])
    sent(gi.at[pl.ds(0, 2)], ys.at[0])
    sent(gi.at[pl.ds(0, 4)], cs.at[0])
    sent(gr.at[pl.ds(0, 7), :, :, 0], gs.at[0])
    sent(gr.at[0, 0, :, 0], gs.at[14])
    sent(gr.at[pl.ds(0, 4)], cs2.at[0])
    sent(mine_r, ys2)
    sent(ksa.at[pl.ds(0, 7)], s_ks.at[0])
    sent(vpa.at[:, pl.ds(0, 896)], s_vp.at[0])
    sent(hid.at[pl.ds(0, 7)], ss.at[14])
    sent(bsend.at[pl.ds(1, 7)], s_key.at[0])
    sent(psend, s_core.at[0])
    sent(ysend, s_y.at[0])
    sent(zb.at[pl.ds(0, 6)], s_z.at[0])
    sent(fb, s_f.at[0])
    sent(mtr, s_mt.at[0])
    sent(vdr, s_vd.at[0])
    vd_add(5, 6, 7)
    vd = SIGMA * jnp.sum(jnp.where(spot, vdt[pl.ds(st, 1)], 0.0), axis=1, keepdims=True)
    for c, w in enumerate(spans):
        total = gathered(0, w) + rn2[0, 0, :, w].astype(F32) + rn2[1, 0, :, w].astype(F32)
        total = total + vd * vsv[:, w].astype(F32)
        arrive(rf.at[:, :, w], s_f.at[3 * c], r_f.at[3 * c], c_dev)
        for k in (0, 1, 2):
            total = total + rf[k, :, w].astype(F32)
        out_ref[:, w] = total.astype(BF)


def store(*refs):
    copies = [pltpu.make_async_copy(a, b, refs[6].at[k]) for k, (a, b) in enumerate(zip(refs[0:3], refs[3:6]))]
    for c in copies:
        c.start()
    for c in copies:
        c.wait()


def body(*args):
    x, kw, vw, kp, ks, vp, vs, fitness = args
    vm = pl.BlockSpec(memory_space=pltpu.VMEM)
    dma = pltpu.SemaphoreType.DMA
    args = (pltpu.with_memory_space_constraint(a, pltpu.HBM) for a in (x, kw.T, vw, kp, ks.T, vp.T, vs, fitness.reshape(1, 16)))
    out, ku, vu = pl.pallas_call(
        kernel,
        out_shape=(
            jax.ShapeDtypeStruct((16, 640), BF),
            jax.ShapeDtypeStruct((320, 640), BF),
            jax.ShapeDtypeStruct((320, 640), BF),
        ),
        in_specs=[pl.BlockSpec(memory_space=pltpu.HBM)] * 8,
        out_specs=(vm, vm, vm),
        scratch_shapes=[
            pltpu.VMEM((320, 640), BF),
            pltpu.VMEM((320, 640), BF),
            pltpu.VMEM((1, 16), BF),
            pltpu.VMEM((16, 640), BF),
            pltpu.VMEM((8, 2, 2, 2, 16, 640), BF),
            pltpu.VMEM((8, 2, 2, 2, 16, 1280), BF),
            pltpu.VMEM((8, 320, 128), BF),
            pltpu.VMEM((320, 1024), BF),
            pltpu.VMEM((8, 320, 128), BF),
            pltpu.VMEM((8, 320, 128), BF),
            pltpu.VMEM((8, 336, 128), BF),
            pltpu.VMEM((320, 1024), BF),
            pltpu.VMEM((8, 2, 2, 2, 16, 640), F32),
            pltpu.VMEM((8, 2, 2, 16, 640), BF),
            pltpu.VMEM((8, 2, 2, 16, 640), BF),
            pltpu.VMEM((8, 2, 16, 640), BF),
            pltpu.VMEM((8, 2, 16, 640), BF),
            pltpu.VMEM((8, 2, 16, 640), F32),
            pltpu.VMEM((8, 2, 16, 640), BF),
            pltpu.VMEM((2, 4, 16, 640), BF),
            pltpu.VMEM((2, 2, 16, 640), BF),
            pltpu.VMEM((3, 16, 640), BF),
            pltpu.VMEM((3, 16, 640), BF),
            pltpu.VMEM((8, 128), F32),
            pltpu.VMEM((4, 8, 128), F32),
            pltpu.VMEM((8, 8, 128), F32),
            pltpu.VMEM((16, 128), F32),
            pltpu.VMEM((4, 16, 128), F32),
            pltpu.VMEM((8, 16, 128), F32),
        ]
        + [dma((n,)) for n in (8, 18, 29, 16, 20, 8, 8)],
        compiler_params=pltpu.CompilerParams(
            collective_id=0, has_side_effects=True, vmem_limit_bytes=48 * 2**20
        ),
        cost_estimate=pl.CostEstimate(flops=1_700_000_000, bytes_accessed=4_000_000, transcendentals=0),
        name="step",
    )(*args)
    anywhere = pl.BlockSpec(memory_space=pl.ANY)
    out, ku, vu = pl.pallas_call(
        store,
        out_shape=tuple(jax.ShapeDtypeStruct(a.shape, BF) for a in (out, ku, vu)),
        in_specs=[anywhere] * 3,
        out_specs=(anywhere,) * 3,
        scratch_shapes=[dma((3,))],
        compiler_params=pltpu.CompilerParams(vmem_limit_bytes=2 * 2**20),
        name="store",
    )(out, ku, vu)
    return out, ku.T, vu


def solution(mesh):
    placed = (
        P("member", "tensor"), P("tensor", "member"), P("member", "tensor"), P("member", "tensor"),
        P("tensor", "member"), P("tensor", "member"), P("member", "tensor"), P("member"),
    )
    return jax.shard_map(
        body,
        mesh=mesh,
        in_specs=placed,
        out_specs=(P("member", "tensor"), P("tensor", "member"), P("member", "tensor")),
        check_vma=False,
    )
```
